128 devices in a mesh: ka: 16 (over z_lo, x, core), band: 8 (over z_hi, y).
Axes of the slice: x: 4, y: 4, z: 4 (z_hi: 2, z_lo: 2; z = z_hi * 2 + z_lo), core: 2. Of those that a mesh axis runs over, the one named last changes fastest.
Arguments:
- orbitals: float32 [16, 64, 2, 4096], P('ka', 'band'), may hold values from -6 to 6
- point_index: int32 [2048], replicated, may hold values from 0 to 4095, as said below
- kernel: bfloat16 [2048, 2048], replicated
- q_weight: float32 [16, 2048], replicated, may hold values from 0.5 to 2
- q_table: int32 [16, 16], replicated, may hold values from 0 to 15
- occ_count: int32 [16], replicated, may hold values from 16 to 64
Outputs:
- exchange: float32 [16, 64, 2, 2048], P(None, 'band', None, 'ka')
The draws below stay inside these ranges and needn't reach their ends.
Inputs may be any that keep to these rules, and one draw needn't show every extreme that they name: point_index[j] is 2 j or 2 j + 1.
All inputs are finite; a program needn't handle non-finite values.
Results may differ from the reference program's by a relative error of at most 0.00049.
Values sent between devices are 32-bit elements; how exact they have to be, the bound alone decides.
No kernel may reach another device: no remote copies, remote signals or barrier semaphores. Data moves between devices by JAX's collectives and lax.ppermute only.
A program may use at most 64 MiB of HBM per device.

```python
import math
import jax
import jax.numpy as jnp
from jax import lax

NMU = 2048
CAND = 4096
NB = 64
K = 16
NQ = 16
STEPS = 3


def draw_point_index(key, part):
    key = jax.random.fold_in(key, 11)
    bits = jax.random.randint(key, (NMU,), 0, 2).astype(jnp.int32)
    bits = bits.at[0].set(0).at[NMU - 1].set(1)
    return (2 * jnp.arange(NMU, dtype=jnp.int32) + bits).astype(jnp.int32)


def draw_kernel(key, part):
    key = jax.random.fold_in(key, 23)
    noise = jax.random.normal(key, (NMU, NMU), jnp.float32)
    spread = 0.6
    sym = (noise + noise.T) * (spread / (2.0 * NMU) ** 0.5)
    return (1.5 * jnp.eye(NMU, dtype=jnp.float32) + sym).astype(jnp.bfloat16)


def draw_occ_count(key, part):
    key = jax.random.fold_in(key, 37)
    first, second = jax.random.split(key)
    counts = jax.random.randint(first, (K,), NB // 4, NB + 1).astype(jnp.int32)
    order = jax.random.permutation(second, K)
    counts = counts.at[order[0]].set(NB).at[order[1]].set(NB // 4)
    return counts.astype(jnp.int32)


def touch_ends(values, own_key, smallest, largest):
    place = [jax.random.randint(jax.random.fold_in(own_key, axis), (), 0, length) for axis, length in enumerate(values.shape)]
    widest = values.shape.index(max(values.shape))
    neighbour = place[:widest] + [(place[widest] + 1) % values.shape[widest]] + place[widest + 1:]
    return values.at[tuple(place)].set(smallest).at[tuple(neighbour)].set(largest)


def block_scale(rng, dims, cuts, smallest, largest):
    level, own = 1.0, jax.random.fold_in(rng, 6)
    for axis_at, parts in cuts:
        steps = jnp.exp(jax.random.uniform(jax.random.fold_in(own, axis_at), (parts,), jnp.float32, smallest / len(cuts), largest / len(cuts)))
        level = level * jnp.repeat(steps, dims[axis_at] // parts).reshape([-1 if axis == axis_at else 1 for axis in range(len(dims))])
    return level


def normal_values(stream_key, extent, scale, bound, pieces=(), held_as=jnp.bfloat16):
    values = jax.random.normal(stream_key, extent, jnp.float32) * scale
    if len(pieces) > 0:
        values = block_scale(stream_key, extent, pieces, -0.22, 0.18) * values
    return jnp.clip(values, min=-bound, max=bound).astype(held_as)


def setup_inputs(seed: int = 0) -> dict:
    splits = jax.random.split(jax.random.key(seed), 7)
    return {
        "orbitals": normal_values(splits[0], (K, NB, 2, CAND), 1.0, 6.0, ((0, 16), (1, 8)), jnp.float32),
        "point_index": draw_point_index(jax.random.fold_in(splits[6], 71), 0),
        "kernel": draw_kernel(jax.random.fold_in(splits[6], 71), 0),
        "q_weight": jnp.clip(jnp.exp(jax.random.uniform(splits[3], (NQ, NMU), jnp.float32, math.log(0.5), math.log(2.0))), 0.5, 2.0),
        "q_table": touch_ends(jax.random.randint(splits[4], (K, K), 0, NQ), jax.random.fold_in(splits[4], 1), 0, NQ - 1).astype(jnp.int32),
        "occ_count": draw_occ_count(jax.random.fold_in(splits[6], 71), 0),
    }


def contribution(mine, other, weight, live, kernel):
    ar = other[:, 0]
    ai = other[:, 1]
    br = mine[:, 0]
    bi = mine[:, 1]
    real_part = br[:, None] * ar[None] + bi[:, None] * ai[None]
    imag_part = ar[None] * bi[:, None] - ai[None] * br[:, None]
    pair = (jnp.stack([real_part, imag_part], axis=2) * weight).astype(jnp.bfloat16)
    width = pair.shape[3]
    flat = pair.reshape(-1, width)
    screened = jnp.dot(flat, kernel, preferred_element_type=jnp.float32).reshape(pair.shape) * weight
    wr = screened[:, :, 0]
    wi = screened[:, :, 1]
    alive = live[None, :, None]
    term_re = lax.optimization_barrier(jnp.sum(alive * (ar[None] * wr - ai[None] * wi), axis=1))
    term_im = lax.optimization_barrier(jnp.sum(alive * (ar[None] * wi + ai[None] * wr), axis=1))
    return jnp.stack([term_re, term_im], axis=1)

def reference(orbitals, point_index, kernel, q_weight, q_table, occ_count):
    points = jnp.take(orbitals, point_index, axis=3)
    count = points.shape[0]
    band_ids = jnp.arange(points.shape[1], dtype=jnp.int32)
    factor = -1.0 / jnp.sqrt(jnp.float32(STEPS * NB))

    def one_point(kidx):
        mine = lax.dynamic_index_in_dim(points, kidx, 0, keepdims=False)
        total = jnp.zeros(mine.shape, jnp.float32)
        for offset in range(STEPS):
            qidx = ((kidx - offset) % count).astype(jnp.int32)
            other = lax.dynamic_index_in_dim(points, qidx, 0, keepdims=False)
            tidx = q_table[kidx, qidx]
            weight = lax.dynamic_index_in_dim(q_weight, tidx, 0, keepdims=False)
            live = (band_ids < occ_count[qidx]).astype(jnp.float32)
            total = total + contribution(mine, other, weight, live, kernel)
        return total * factor
    return lax.map(one_point, jnp.arange(count, dtype=jnp.int32))
```

```python
import jax
import jax.numpy as jnp
from jax import lax
from jax.experimental import pallas as pl
from jax.experimental.pallas import tpu as pltpu
from jax.sharding import PartitionSpec as P

STEPS = 3
KPTS = 16
BLOCKS = 8
ROWS = 16
POINTS = 2048
HALF = POINTS // 2
TILE = 256
DEPTH = 128
FACTOR = -1.0 / (STEPS * 64) ** 0.5
F32, BF16 = jnp.float32, jnp.bfloat16


def device(i, c, zh, y):
    return ((i % 8) * 2 + c) * BLOCKS + zh * 4 + y % 4


def everyone():
    return [(i, c, zh, y) for i in range(8) for c in range(2) for zh in range(2) for y in range(4)]


def gather_pairs(tz, ty):
    pairs = []
    for i, c, zh, y in everyone():
        if y % 2 == c:
            to = device(i, c, zh ^ tz, y + 2 * ty)
        else:
            to = device(i, 1 - c, zh ^ tz, y + 1 + 2 * ty)
        pairs.append((device(i, c, zh, y), to))
    return pairs


def own_band_pairs():
    pairs = []
    for i, c, zh, y in everyone():
        stay = c == 0 and y % 2 == 1
        pairs.append((device(i, c, zh, y), device(i if stay else i + 1, c, zh, y)))
    return pairs


def next_band_pairs():
    pairs = []
    for i, c, zh, y in everyone():
        stay = c == 0 and y % 2 == 0
        pairs.append((device(i, c, zh, y), device(i if stay else i + 1, c, zh, y ^ 1)))
    return pairs


def core_pairs():
    return [(device(i, c, zh, y), device(i, 1 - c, zh, y)) for i, c, zh, y in everyone()]


def send(value, pairs):
    return lax.ppermute(value, ("ka", "band"), pairs)


def place():
    ka, band = lax.axis_index("ka"), lax.axis_index("band")
    return ka // 2, ka % 2, band // 4, band % 4, band


def pick_kernel(index_ref, orb_ref, out_ref):
    for j in range(POINTS // 128):
        idx = jnp.broadcast_to(index_ref[:, j * 128 : (j + 1) * 128], (8, 128)) & 127
        low = lax.broadcasted_iota(jnp.int32, (8, 128), 1) < 64
        for part in range(2):
            left = orb_ref[:, part, 2 * j * 128 : (2 * j + 1) * 128]
            right = orb_ref[:, part, (2 * j + 1) * 128 : (2 * j + 2) * 128]
            got = jnp.where(
                low,
                jnp.take_along_axis(left, idx, axis=1, mode="promise_in_bounds"),
                jnp.take_along_axis(right, idx, axis=1, mode="promise_in_bounds"),
            )
            out_ref[part * 8 : part * 8 + 8, j * 128 : (j + 1) * 128] = got


def pick(orbitals, point_index):
    return pl.pallas_call(
        pick_kernel,
        out_shape=jax.ShapeDtypeStruct((ROWS, POINTS), F32),
        name="pick_points",
    )(point_index.reshape(1, POINTS), orbitals)


def halves(value, c):
    out = []
    for j in range(value.shape[1] // 256):
        a, b = value[:, j * 256 : j * 256 + 128], value[:, j * 256 + 128 : j * 256 + 256]
        low = lax.broadcasted_iota(jnp.int32, a.shape, 1) < 64
        first = jnp.where(c == 0, a, pltpu.roll(a, 64, 1))
        second = jnp.where(c == 0, pltpu.roll(b, 64, 1), b)
        out.append(jnp.where(low, first, second))
    return jnp.concatenate(out, axis=1)


def columns_kernel(k_ref, out_ref):
    c = place()[1]
    out_ref[...] = halves(k_ref[...].astype(F32), c).astype(BF16)


def columns(kernel):
    rows = 256
    return pl.pallas_call(
        columns_kernel,
        grid=(POINTS // rows,),
        in_specs=[pl.BlockSpec((rows, POINTS), lambda r: (r, 0))],
        out_specs=pl.BlockSpec((rows, HALF), lambda r: (r, 0)),
        out_shape=jax.ShapeDtypeStruct((POINTS, HALF), BF16),
        cost_estimate=pl.CostEstimate(flops=POINTS * POINTS * 4, bytes_accessed=12 * 2**20, transcendentals=0),
        name="kernel_columns",
    )(kernel)


def split(value):
    high = value.astype(BF16)
    return high, (value - high.astype(F32)).astype(BF16)


def exchange_kernel(table_ref, occ_ref, weight_ref, k_ref, *refs):
    mine, theirs = refs[0:4], refs[4:8]
    before = refs[8:12]
    out_ref = refs[12]
    x_ref, xcat_ref, p_ref, pt_ref, f_ref, mhi_ref, mlo_ref = refs[13:]
    i, c, zh, y, band = place()
    parity = y % 2
    kpoint = 2 * i + parity
    same = c == parity
    own_step = jnp.where(same, 2, 1)
    steps = (0, own_step, 3 - own_step)
    points = [lax.rem(kpoint - s + KPTS, KPTS) for s in steps]

    @pl.when(pl.program_id(0) == 0)
    def _():
        for group, shift in ((mine, jnp.where(same, 0, 1)), (theirs, jnp.where(same, 1, 0))):
            for t, ref in enumerate(group):
                tz, ty = t // 2, t % 2
                block = jnp.where(zh == tz, 0, 4) + lax.rem(y - shift - 2 * ty + 8, 4)
                value = ref[...]
                x_ref[block] = value
                high, low = split(value)
                row = pl.multiple_of(block * ROWS, ROWS)
                xcat_ref[pl.ds(row, ROWS), :] = high
                xcat_ref[pl.ds(pl.multiple_of(128 + row, ROWS), ROWS), :] = low
        f_ref[...] = jnp.zeros_like(f_ref)
        for g in range(STEPS):
            f_ref[pl.ds(g, 1), :] = weight_ref[pl.ds(table_ref[kpoint, points[g]], 1), :]
        p_ref[96:, :] = jnp.zeros((DEPTH - 96, POINTS), F32)
        p_ref[0:16, :] = x_ref[band]
        p_ref[16:32, :] = x_ref[band ^ 1]
        for n in range(4):
            p_ref[32 + 16 * n : 48 + 16 * n, :] = before[n][...]
        for j in range(POINTS // 128):
            cols = slice(j * 128, (j + 1) * 128)
            scaled = jnp.concatenate(
                [p_ref[32 * g : 32 * g + 32, cols] * f_ref[g : g + 1, cols] for g in range(STEPS)] + [p_ref[96:, cols]], axis=0
            )
            high, low = split(scaled.T)
            pt_ref[cols, 0:128] = high
            pt_ref[cols, 128:256] = high
            pt_ref[cols, 256:384] = low

    start = pl.multiple_of(pl.program_id(0) * 2 * TILE, 2 * TILE)
    f_here = halves(f_ref[:, pl.ds(start, 2 * TILE)], c)
    row = lax.broadcasted_iota(jnp.int32, (32, TILE), 0)
    number = jnp.where(row < 16, band, band ^ 1) * 8 + (row & 7)
    plain, turned = [], []
    for g in range(STEPS):
        live = number < occ_ref[points[g]]
        value = halves(p_ref[32 * g : 32 * g + 32, pl.ds(start, 2 * TILE)], c) * f_here[g : g + 1]
        value = jnp.where(live, value, 0.0)
        plain.append(value)
        turned += [value[8:16], -value[0:8], value[24:32], -value[16:24]]
    fill = [jnp.zeros((DEPTH - 96, TILE), F32)]
    both = jnp.concatenate([jnp.concatenate(plain + fill, axis=0), jnp.concatenate(turned + fill, axis=0)], axis=1)
    high, low = split(both)
    w = jnp.concatenate([high, low, high], axis=0)
    chunk = 512
    for n in range(POINTS // chunk):
        rows = slice(n * chunk, (n + 1) * chunk)
        e = jnp.dot(pt_ref[rows, :], w, preferred_element_type=F32)
        kf = k_ref[rows, :].astype(F32)
        for part in range(2):
            cols = slice(part * TILE, (part + 1) * TILE)
            high, low = split(e[:, cols] * kf)
            mhi_ref[rows, cols] = high
            mlo_ref[rows, cols] = low
    first = jnp.dot(xcat_ref[...], mhi_ref[...], preferred_element_type=F32)
    second = jnp.dot(xcat_ref[0:128, :], mlo_ref[...], preferred_element_type=F32)
    r = first[0:128] + first[128:256] + second
    low_lanes = lax.broadcasted_iota(jnp.int32, (8, 128), 1) < 64
    for b in range(BLOCKS):
        top, bottom = r[b * ROWS : b * ROWS + 8], r[b * ROWS + 8 : b * ROWS + 16]
        re = top[:, :TILE] - bottom[:, TILE:]
        im = top[:, TILE:] + bottom[:, :TILE]
        for j in range(TILE // 128):
            a, d = re[:, j * 128 : (j + 1) * 128], im[:, j * 128 : (j + 1) * 128]
            out_ref[2 * j, b] = jnp.where(low_lanes, a, pltpu.roll(d, 64, 1))
            out_ref[2 * j + 1, b] = jnp.where(low_lanes, pltpu.roll(a, 64, 1), d)


def exchange(q_table, occ_count, q_weight, half_kernel, mine, theirs, before):
    whole = pl.BlockSpec(memory_space=pltpu.VMEM)
    smem = pl.BlockSpec(memory_space=pltpu.SMEM)
    return pl.pallas_call(
        exchange_kernel,
        grid=(HALF // TILE,),
        in_specs=[smem, smem, whole, pl.BlockSpec((POINTS, TILE), lambda u: (0, u))] + [whole] * 12,
        out_specs=pl.BlockSpec((4, BLOCKS, 8, 128), lambda u: (u, 0, 0, 0)),
        out_shape=jax.ShapeDtypeStruct((KPTS, BLOCKS, 8, 128), F32),
        scratch_shapes=[
            pltpu.VMEM((BLOCKS, ROWS, POINTS), F32),
            pltpu.VMEM((256, POINTS), BF16),
            pltpu.VMEM((DEPTH, POINTS), F32),
            pltpu.VMEM((POINTS, 3 * DEPTH), BF16),
            pltpu.VMEM((8, POINTS), F32),
            pltpu.VMEM((POINTS, 2 * TILE), BF16),
            pltpu.VMEM((POINTS, 2 * TILE), BF16),
        ],
        compiler_params=pltpu.CompilerParams(vmem_limit_bytes=40 * 2**20),
        cost_estimate=pl.CostEstimate(flops=14 * 10**9, bytes_accessed=8 * 2**20, transcendentals=0),
        name="exchange_terms",
    )(q_table, occ_count, q_weight, half_kernel, *mine, *theirs, *before)


def total_kernel(in_ref, out_ref):
    low = lax.broadcasted_iota(jnp.int32, (8, 128), 1) < 64
    for k in range(KPTS):
        i, parity = k // 2, k % 2
        sums = []
        for c in range(2):
            parts = [in_ref[device(i, c, zh, parity + 2 * h)] for zh in range(2) for h in range(2)]
            sums.append(((parts[0] + parts[1]) + (parts[2] + parts[3])) * FACTOR)
        out_ref[k, :, 0, :] = jnp.where(low, sums[0], pltpu.roll(sums[1], 64, 1))
        out_ref[k, :, 1, :] = jnp.where(low, pltpu.roll(sums[0], 64, 1), sums[1])


def total(parts):
    return pl.pallas_call(
        total_kernel,
        out_shape=jax.ShapeDtypeStruct((KPTS, 8, 2, 128), F32),
        name="total",
    )(parts)


def body(orbitals, point_index, kernel, q_weight, q_table, occ_count):
    block = pick(orbitals[0], point_index)
    mine = [send(block, gather_pairs(t // 2, t % 2)) for t in range(4)]
    before = [send(block, own_band_pairs()), send(block, next_band_pairs())]
    theirs = [send(value, core_pairs()) for value in mine]
    before_theirs = [send(value, core_pairs()) for value in before]
    half_kernel = columns(kernel)
    parts = exchange(q_table, occ_count, q_weight, half_kernel, mine, theirs, before + before_theirs)
    got = lax.all_to_all(parts.reshape(128, 8, 128), ("ka", "band"), 0, 0, tiled=True)
    return total(got)


def solution(mesh):
    placed = (P("ka", "band", None, None), P(), P(), P(), P(), P())
    return jax.shard_map(body, mesh=mesh, in_specs=placed, out_specs=P(None, "band", None, "ka"), check_vma=False)
```

```python
import jax
import jax.numpy as jnp
from jax import lax
from jax.experimental import pallas as pl
from jax.experimental.pallas import tpu as pltpu
from jax.sharding import Mesh
from jax.sharding import PartitionSpec as P

STEPS = 3
KPTS = 16
BLOCKS = 8
ROWS = 16
POINTS = 2048
TILES = 4
WIDE = 2
DEPTH = 128
CHUNK = 256
FACTOR = -1.0 / (STEPS * 64) ** 0.5
F32, BF16 = jnp.float32, jnp.bfloat16


def device(i, c, zh, y):
    return ((i % 8) * 2 + c) * BLOCKS + zh * 4 + y % 4


def everyone():
    return [(i, c, zh, y) for i in range(8) for c in range(2) for zh in range(2) for y in range(4)]


def gather_pairs(tz, ty):
    pairs = []
    for i, c, zh, y in everyone():
        if y % 2 == c:
            to = device(i, c, zh ^ tz, y + 2 * ty)
        else:
            to = device(i, 1 - c, zh ^ tz, (y ^ 1) + 2 * ty)
        pairs.append((device(i, c, zh, y), to))
    return pairs


def own_band_pairs():
    pairs = []
    for i, c, zh, y in everyone():
        stay = c == 0 and y % 2 == 1
        pairs.append((device(i, c, zh, y), device(i if stay else i + 1, c, zh, y)))
    return pairs


def next_band_pairs():
    pairs = []
    for i, c, zh, y in everyone():
        stay = c == 0 and y % 2 == 0
        pairs.append((device(i, c, zh, y), device(i if stay else i + 1, c, zh, y ^ 1)))
    return pairs


def core_pairs():
    return [(device(i, c, zh, y), device(i, 1 - c, zh, y)) for i, c, zh, y in everyone()]


def send(value, pairs):
    return lax.ppermute(value, ("i", "core", "band"), pairs)


def place():
    band = lax.axis_index("band")
    return lax.axis_index("i"), lax.axis_index("core"), band // 4, band % 4, band


def pick_kernel(index_ref, orb_ref, out_ref):
    for j in range(POINTS // 128):
        idx = jnp.broadcast_to(index_ref[:, j * 128 : (j + 1) * 128], (8, 128)) & 127
        low = lax.broadcasted_iota(jnp.int32, (8, 128), 1) < 64
        for part in range(2):
            left = orb_ref[:, part, 2 * j * 128 : (2 * j + 1) * 128]
            right = orb_ref[:, part, (2 * j + 1) * 128 : (2 * j + 2) * 128]
            got = jnp.where(
                low,
                jnp.take_along_axis(left, idx, axis=1, mode="promise_in_bounds"),
                jnp.take_along_axis(right, idx, axis=1, mode="promise_in_bounds"),
            )
            out_ref[part * 8 : part * 8 + 8, j * 128 : (j + 1) * 128] = got


def pick(orbitals, point_index):
    return pl.pallas_call(
        pick_kernel,
        out_shape=jax.ShapeDtypeStruct((ROWS, POINTS), F32),
        name="pick_points",
    )(point_index.reshape(1, POINTS), orbitals)


def split(value):
    high = value.astype(BF16)
    return high, (value - high.astype(F32)).astype(BF16)


def product_kernel(core_ref, table_ref, occ_ref, weight_ref, *refs):
    k_refs, refs = refs[:WIDE], refs[WIDE:]
    mine, theirs, before = refs[0], refs[1], refs[2:6]
    high_ref, low_ref, p_ref, pt_ref, f_ref = refs[6:]
    i, c, zh, y, band = place()
    parity = y % 2
    kpoint = 2 * i + parity
    same = c == parity
    own_step = jnp.where(same, 2, 1)
    points = [lax.rem(kpoint - s + KPTS, KPTS) for s in (0, own_step, 3 - own_step)]

    @pl.when(pl.program_id(0) == 0)
    def _():
        f_ref[...] = jnp.zeros_like(f_ref)
        for g in range(STEPS):
            f_ref[pl.ds(g, 1), :] = weight_ref[pl.ds(table_ref[kpoint, points[g]], 1), :]
        p_ref[96:, :] = jnp.zeros((DEPTH - 96, POINTS), F32)
        p_ref[0:16, :] = jnp.where(same, mine[...], theirs[...])
        p_ref[16:32, :] = jnp.where(same, theirs[...], mine[...])
        for n in range(4):
            p_ref[32 + 16 * n : 48 + 16 * n, :] = before[n][...]
        for j in range(POINTS // 128):
            cols = slice(j * 128, (j + 1) * 128)
            scaled = jnp.concatenate(
                [p_ref[32 * g : 32 * g + 32, cols] * f_ref[g : g + 1, cols] for g in range(STEPS)] + [p_ref[96:, cols]], axis=0
            )
            high, low = split(scaled.T)
            pt_ref[cols, 0:128] = high
            pt_ref[cols, 128:256] = high
            pt_ref[cols, 256:384] = low

    row = lax.broadcasted_iota(jnp.int32, (32, 128), 0)
    number = jnp.where(row < 16, band, band ^ 1) * 8 + (row & 7)
    fill = [jnp.zeros((DEPTH - 96, 128), F32)]
    sides = []
    for j in range(WIDE):
        here = pl.ds(pl.multiple_of((2 * (pl.program_id(0) * WIDE + j) + c) * 128, 128), 128)
        f_here = f_ref[:, here]
        plain, turned = [], []
        for g in range(STEPS):
            live = number < occ_ref[points[g]]
            value = jnp.where(live, p_ref[32 * g : 32 * g + 32, here] * f_here[g : g + 1], 0.0)
            plain.append(value)
            turned += [value[8:16], -value[0:8], value[24:32], -value[16:24]]
        sides += [jnp.concatenate(plain + fill, axis=0), jnp.concatenate(turned + fill, axis=0)]
    high, low = split(jnp.concatenate(sides, axis=1))
    w = jnp.concatenate([high, low, high], axis=0)
    for n in range(POINTS // CHUNK):
        rows = slice(n * CHUNK, (n + 1) * CHUNK)
        e = jnp.dot(pt_ref[rows, :], w, preferred_element_type=F32)
        for j in range(WIDE):
            kf = k_refs[j][rows, :].astype(F32)
            for part in range(2):
                cols = slice((2 * j + part) * 128, (2 * j + part + 1) * 128)
                high, low = split(e[:, cols] * kf)
                high_ref[pl.program_id(0), rows, cols] = high
                low_ref[pl.program_id(0), rows, cols] = low


WHOLE = pl.BlockSpec(memory_space=pltpu.VMEM)
SMEM = pl.BlockSpec(memory_space=pltpu.SMEM)


def product(core, q_table, occ_count, q_weight, kernel, mine, theirs, before):
    return pl.pallas_call(
        product_kernel,
        grid_spec=pltpu.PrefetchScalarGridSpec(
            num_scalar_prefetch=1,
            grid=(TILES,),
            in_specs=[SMEM, SMEM, WHOLE]
            + [pl.BlockSpec((POINTS, 128), lambda u, core, j=j: (0, 2 * (u * WIDE + j) + core[0])) for j in range(WIDE)]
            + [WHOLE] * 6,
            out_specs=[WHOLE, WHOLE],
            scratch_shapes=[
                pltpu.VMEM((DEPTH, POINTS), F32),
                pltpu.VMEM((POINTS, 3 * DEPTH), BF16),
                pltpu.VMEM((8, POINTS), F32),
            ],
        ),
        out_shape=[jax.ShapeDtypeStruct((TILES, POINTS, WIDE * 256), BF16)] * 2,
        compiler_params=pltpu.CompilerParams(vmem_limit_bytes=28 * 2**20),
        cost_estimate=pl.CostEstimate(flops=7 * 10**9, bytes_accessed=8 * 2**20, transcendentals=0),
        name="kernel_product",
    )(core, q_table, occ_count, q_weight, *[kernel] * WIDE, mine, theirs, *before)


def apply_kernel(high_ref, low_ref, *refs):
    mine, theirs, out_ref, x_ref = refs[0:4], refs[4:8], refs[8], refs[9]
    i, c, zh, y, band = place()
    same = c == y % 2
    for group, first in ((mine, jnp.where(same, band, band ^ 1)), (theirs, jnp.where(same, band ^ 1, band))):
        for t, ref in enumerate(group):
            block = first ^ (4 * (t // 2) + 2 * (t % 2))
            high, low = split(ref[...])
            row = pl.multiple_of(block * ROWS, ROWS)
            x_ref[pl.ds(row, ROWS), :] = high
            x_ref[pl.ds(pl.multiple_of(128 + row, ROWS), ROWS), :] = low
    for u in range(TILES):
        first = jnp.dot(x_ref[...], high_ref[u], preferred_element_type=F32)
        second = jnp.dot(x_ref[0:128, :], low_ref[u], preferred_element_type=F32)
        r = first[0:128] + first[128:256] + second
        for b in range(BLOCKS):
            top, bottom = r[b * ROWS : b * ROWS + 8], r[b * ROWS + 8 : b * ROWS + 16]
            for j in range(WIDE):
                re, im = slice(j * 256, j * 256 + 128), slice(j * 256 + 128, j * 256 + 256)
                out_ref[u * WIDE + j, b, 0] = top[:, re] - bottom[:, im]
                out_ref[u * WIDE + j, b, 1] = top[:, im] + bottom[:, re]


def apply(high, low, mine, theirs):
    return pl.pallas_call(
        apply_kernel,
        in_specs=[WHOLE] * 10,
        out_specs=WHOLE,
        out_shape=jax.ShapeDtypeStruct((TILES * WIDE, BLOCKS, 2, 8, 128), F32),
        scratch_shapes=[pltpu.VMEM((256, POINTS), BF16)],
        compiler_params=pltpu.CompilerParams(vmem_limit_bytes=28 * 2**20),
        cost_estimate=pl.CostEstimate(flops=4 * 10**9, bytes_accessed=18 * 2**20, transcendentals=0),
        name="apply_orbitals",
    )(high, low, *mine, *theirs)


def total_kernel(in_ref, out_ref):
    for k in range(KPTS):
        i, parity = k // 2, k % 2
        for part in range(2):
            parts = [in_ref[i * BLOCKS + zh * 4 + parity + 2 * h, part] for zh in range(2) for h in range(2)]
            out_ref[k, :, part, :] = ((parts[0] + parts[1]) + (parts[2] + parts[3])) * FACTOR


def total(parts):
    return pl.pallas_call(
        total_kernel,
        out_shape=jax.ShapeDtypeStruct((KPTS, 8, 2, 128), F32),
        name="total",
    )(parts)


def body(orbitals, point_index, kernel, q_weight, q_table, occ_count):
    core = lax.axis_index("core").astype(jnp.int32).reshape(1)
    kernel, q_weight, q_table, occ_count = (
        pltpu.with_memory_space_constraint(value, pltpu.HBM) for value in (kernel, q_weight, q_table, occ_count)
    )
    block = pick(orbitals[0], point_index)
    far = [send(block, gather_pairs(1, t)) for t in range(2)]
    near = [send(block, gather_pairs(0, t)) for t in range(2)]
    before = [send(block, own_band_pairs()), send(block, next_band_pairs())]
    before_theirs = [send(value, core_pairs()) for value in before]
    near_theirs = [send(value, core_pairs()) for value in near]
    high, low = product(core, q_table, occ_count, q_weight, kernel, near[0], near_theirs[0], before + before_theirs)
    far[0], far[1], high, low = lax.optimization_barrier((far[0], far[1], high, low))
    far_theirs = [send(value, core_pairs()) for value in far]
    parts = apply(high, low, near + far, near_theirs + far_theirs)
    got = lax.all_to_all(parts.reshape(64, 2, 8, 128), ("i", "band"), 0, 0, tiled=True)
    return total(got)


def solution(mesh):
    split_mesh = Mesh(mesh.devices.reshape(8, 2, BLOCKS), ("i", "core", "band"))
    ka = ("i", "core")
    placed = (P(ka, "band", None, None), P(), P(), P(), P(), P())
    return jax.shard_map(body, mesh=split_mesh, in_specs=placed, out_specs=P(None, "band", None, ka), check_vma=False)
```

```python
import jax
import jax.numpy as jnp
from jax import lax
from jax.experimental import pallas as pl
from jax.experimental.pallas import tpu as pltpu
from jax.sharding import Mesh
from jax.sharding import PartitionSpec as P

STEPS = 3
KPTS = 16
BLOCKS = 8
ROWS = 16
POINTS = 2048
TILES = 4
WIDE = 2
DEPTH = 256
CHUNK = 512
FACTOR = -1.0 / (STEPS * 64) ** 0.5
F32, BF16 = jnp.float32, jnp.bfloat16


def device(i, c, zh, y):
    return ((i % 8) * 2 + c) * BLOCKS + zh * 4 + y % 4


def everyone():
    return [(i, c, zh, y) for i in range(8) for c in range(2) for zh in range(2) for y in range(4)]


def gather_pairs(tz, ty):
    pairs = []
    for i, c, zh, y in everyone():
        if y % 2 == c:
            to = device(i, c, zh ^ tz, y + 2 * ty)
        else:
            to = device(i, 1 - c, zh ^ tz, (y ^ 1) + 2 * ty)
        pairs.append((device(i, c, zh, y), to))
    return pairs


def own_band_pairs():
    pairs = []
    for i, c, zh, y in everyone():
        stay = c == 0 and y % 2 == 1
        pairs.append((device(i, c, zh, y), device(i if stay else i + 1, c, zh, y)))
    return pairs


def next_band_pairs():
    pairs = []
    for i, c, zh, y in everyone():
        stay = c == 0 and y % 2 == 0
        pairs.append((device(i, c, zh, y), device(i if stay else i + 1, c, zh, y ^ 1)))
    return pairs


def core_pairs():
    return [(device(i, c, zh, y), device(i, 1 - c, zh, y)) for i, c, zh, y in everyone()]


def send(value, pairs):
    return lax.ppermute(value, ("i", "core", "band"), pairs)


def place():
    band = lax.axis_index("band")
    return lax.axis_index("i"), lax.axis_index("core"), band // 4, band % 4, band


def pick_kernel(index_ref, orb_ref, out_ref):
    for j in range(POINTS // 128):
        idx = jnp.broadcast_to(index_ref[:, j * 128 : (j + 1) * 128], (8, 128)) & 127
        low = lax.broadcasted_iota(jnp.int32, (8, 128), 1) < 64
        for part in range(2):
            left = orb_ref[:, part, 2 * j * 128 : (2 * j + 1) * 128]
            right = orb_ref[:, part, (2 * j + 1) * 128 : (2 * j + 2) * 128]
            got = jnp.where(
                low,
                jnp.take_along_axis(left, idx, axis=1, mode="promise_in_bounds"),
                jnp.take_along_axis(right, idx, axis=1, mode="promise_in_bounds"),
            )
            out_ref[part * 8 : part * 8 + 8, j * 128 : (j + 1) * 128] = got


def pick(orbitals, point_index):
    return pl.pallas_call(
        pick_kernel,
        out_shape=pltpu.VMEM((ROWS, POINTS), F32),
        name="pick_points",
    )(point_index.reshape(1, POINTS), orbitals)


def split(value):
    high = value.astype(BF16)
    return high, (value - high.astype(F32)).astype(BF16)


def product_kernel(core_ref, table_ref, occ_ref, weight_ref, *refs):
    k_refs, refs = refs[:WIDE], refs[WIDE:]
    mine, theirs, before = refs[0], refs[1], refs[2:6]
    high_ref, low_ref, p_ref, pt_ref, f_ref = refs[6:]
    i, c, zh, y, band = place()
    parity = y % 2
    kpoint = 2 * i + parity
    same = c == parity
    own_step = jnp.where(same, 2, 1)
    points = [lax.rem(kpoint - s + KPTS, KPTS) for s in (0, own_step, 3 - own_step)]

    @pl.when(pl.program_id(0) == 0)
    def _():
        f_ref[...] = jnp.zeros_like(f_ref)
        for g in range(STEPS):
            f_ref[pl.ds(g, 1), :] = weight_ref[pl.ds(table_ref[kpoint, points[g]], 1), :]
        p_ref[0:16, :] = jnp.where(same, mine[...], theirs[...])
        p_ref[16:32, :] = jnp.where(same, theirs[...], mine[...])
        for n in range(4):
            p_ref[32 + 16 * n : 48 + 16 * n, :] = before[n][...]
        for j in range(POINTS // 128):
            cols = slice(j * 128, (j + 1) * 128)
            scaled = jnp.concatenate([p_ref[32 * g : 32 * g + 32, cols] * f_ref[g : g + 1, cols] for g in range(STEPS)], axis=0)
            high = scaled.astype(BF16).astype(F32)
            pt_ref[cols, :] = jnp.concatenate([high, high, (scaled - high)[0:64]], axis=0).T.astype(BF16)

    row = lax.broadcasted_iota(jnp.int32, (32, 128), 0)
    number = jnp.where(row < 16, band, band ^ 1) * 8 + (row & 7)
    sides = []
    for j in range(WIDE):
        here = pl.ds(pl.multiple_of((2 * (pl.program_id(0) * WIDE + j) + c) * 128, 128), 128)
        f_here = f_ref[:, here]
        plain, turned = [], []
        for g in range(STEPS):
            live = number < occ_ref[points[g]]
            value = jnp.where(live, p_ref[32 * g : 32 * g + 32, here] * f_here[g : g + 1], 0.0)
            plain.append(value)
            turned += [value[8:16], -value[0:8], value[24:32], -value[16:24]]
        sides += [jnp.concatenate(plain, axis=0), jnp.concatenate(turned, axis=0)]
    high, low = split(jnp.concatenate(sides, axis=1))
    w = jnp.concatenate([high, low, high[0:64]], axis=0)
    for n in range(POINTS // CHUNK):
        rows = slice(n * CHUNK, (n + 1) * CHUNK)
        e = jnp.dot(pt_ref[rows, :], w, preferred_element_type=F32)
        for j in range(WIDE):
            kf = k_refs[j][rows, :].astype(F32)
            for part in range(2):
                cols = slice((2 * j + part) * 128, (2 * j + part + 1) * 128)
                high, low = split(e[:, cols] * kf)
                high_ref[pl.program_id(0), rows, cols] = high
                low_ref[pl.program_id(0), rows, cols] = low


WHOLE = pl.BlockSpec(memory_space=pltpu.VMEM)
SMEM = pl.BlockSpec(memory_space=pltpu.SMEM)


def product(core, q_table, occ_count, q_weight, kernel, mine, theirs, before):
    return pl.pallas_call(
        product_kernel,
        grid_spec=pltpu.PrefetchScalarGridSpec(
            num_scalar_prefetch=1,
            grid=(TILES,),
            in_specs=[SMEM, SMEM, WHOLE]
            + [pl.BlockSpec((POINTS, 128), lambda u, core, j=j: (0, 2 * (u * WIDE + j) + core[0])) for j in range(WIDE)]
            + [WHOLE] * 6,
            out_specs=[WHOLE, WHOLE],
            scratch_shapes=[
                pltpu.VMEM((32 * STEPS, POINTS), F32),
                pltpu.VMEM((POINTS, DEPTH), BF16),
                pltpu.VMEM((8, POINTS), F32),
            ],
        ),
        out_shape=[jax.ShapeDtypeStruct((TILES, POINTS, WIDE * 256), BF16)] * 2,
        compiler_params=pltpu.CompilerParams(vmem_limit_bytes=28 * 2**20),
        cost_estimate=pl.CostEstimate(flops=7 * 10**9, bytes_accessed=8 * 2**20, transcendentals=0),
        name="kernel_product",
    )(core, q_table, occ_count, q_weight, *[kernel] * WIDE, mine, theirs, *before)


def apply_kernel(high_ref, low_ref, *refs):
    mine, theirs, out_ref, x_ref = refs[0:4], refs[4:8], refs[8], refs[9]
    i, c, zh, y, band = place()
    same = c == y % 2
    for group, first in ((mine, jnp.where(same, band, band ^ 1)), (theirs, jnp.where(same, band ^ 1, band))):
        for t, ref in enumerate(group):
            block = first ^ (4 * (t // 2) + 2 * (t % 2))
            high, low = split(ref[...])
            row = pl.multiple_of(block * ROWS, ROWS)
            x_ref[pl.ds(row, ROWS), :] = high
            x_ref[pl.ds(pl.multiple_of(128 + row, ROWS), ROWS), :] = low
    for u in range(TILES):
        first = jnp.dot(x_ref[...], high_ref[u], preferred_element_type=F32)
        second = jnp.dot(x_ref[0:128, :], low_ref[u], preferred_element_type=F32)
        r = first[0:128] + first[128:256] + second
        for b in range(BLOCKS):
            top, bottom = r[b * ROWS : b * ROWS + 8], r[b * ROWS + 8 : b * ROWS + 16]
            for j in range(WIDE):
                re, im = slice(j * 256, j * 256 + 128), slice(j * 256 + 128, j * 256 + 256)
                out_ref[u * WIDE + j, b, 0] = top[:, re] - bottom[:, im]
                out_ref[u * WIDE + j, b, 1] = top[:, im] + bottom[:, re]


def apply(high, low, mine, theirs):
    return pl.pallas_call(
        apply_kernel,
        in_specs=[WHOLE] * 10,
        out_specs=WHOLE,
        out_shape=jax.ShapeDtypeStruct((TILES * WIDE, BLOCKS, 2, 8, 128), F32),
        scratch_shapes=[pltpu.VMEM((256, POINTS), BF16)],
        compiler_params=pltpu.CompilerParams(vmem_limit_bytes=28 * 2**20),
        cost_estimate=pl.CostEstimate(flops=4 * 10**9, bytes_accessed=18 * 2**20, transcendentals=0),
        name="apply_orbitals",
    )(high, low, *mine, *theirs)


def total_kernel(in_ref, out_ref):
    for k in range(KPTS):
        i, parity = k // 2, k % 2
        for part in range(2):
            parts = [in_ref[i * BLOCKS + zh * 4 + parity + 2 * h, part] for zh in range(2) for h in range(2)]
            out_ref[k, :, part, :] = ((parts[0] + parts[1]) + (parts[2] + parts[3])) * FACTOR


def total(parts):
    return pl.pallas_call(
        total_kernel,
        out_shape=jax.ShapeDtypeStruct((KPTS, 8, 2, 128), F32),
        name="total",
    )(pltpu.with_memory_space_constraint(parts, pltpu.VMEM))


def body(orbitals, point_index, kernel, q_weight, q_table, occ_count):
    core = lax.axis_index("core").astype(jnp.int32).reshape(1)
    kernel, q_weight, q_table, occ_count = (
        pltpu.with_memory_space_constraint(value, pltpu.HBM) for value in (kernel, q_weight, q_table, occ_count)
    )
    block = pick(orbitals[0], point_index)
    far = [send(block, gather_pairs(1, t)) for t in range(2)]
    near = [send(block, gather_pairs(0, t)) for t in range(2)]
    before = [send(block, own_band_pairs()), send(block, next_band_pairs())]
    before[0], before[1], near[0] = lax.optimization_barrier((before[0], before[1], near[0]))
    before_theirs = [send(value, core_pairs()) for value in before]
    near_theirs = [send(value, core_pairs()) for value in near]
    high, low = product(core, q_table, occ_count, q_weight, kernel, near[0], near_theirs[0], before + before_theirs)
    far[0], far[1], high, low = lax.optimization_barrier((far[0], far[1], high, low))
    far_theirs = [send(value, core_pairs()) for value in far]
    parts = apply(high, low, near + far, near_theirs + far_theirs)
    got = lax.all_to_all(parts.reshape(64, 2, 8, 128), ("i", "band"), 0, 0, tiled=True)
    return total(got)


def solution(mesh):
    split_mesh = Mesh(mesh.devices.reshape(8, 2, BLOCKS), ("i", "core", "band"))
    ka = ("i", "core")
    placed = (P(ka, "band", None, None), P(), P(), P(), P(), P())
    return jax.shard_map(body, mesh=split_mesh, in_specs=placed, out_specs=P(None, "band", None, ka), check_vma=False)
```

```python
import jax
import jax.numpy as jnp
from jax import lax
from jax.experimental import pallas as pl
from jax.experimental.pallas import tpu as pltpu
from jax.sharding import Mesh
from jax.sharding import PartitionSpec as P

STEPS = 3
KPTS = 16
BLOCKS = 8
ROWS = 16
POINTS = 2048
TILES = 4
WIDE = 2
DEPTH = 256
CHUNK = 512
FACTOR = -1.0 / (STEPS * 64) ** 0.5
F32, BF16 = jnp.float32, jnp.bfloat16


def device(i, c, zh, y):
    return ((i % 8) * 2 + c) * BLOCKS + zh * 4 + y % 4


def everyone():
    return [(i, c, zh, y) for i in range(8) for c in range(2) for zh in range(2) for y in range(4)]


def gather_pairs(tz, ty):
    pairs = []
    for i, c, zh, y in everyone():
        if y % 2 == c:
            to = device(i, c, zh ^ tz, y + 2 * ty)
        else:
            to = device(i, 1 - c, zh ^ tz, (y ^ 1) + 2 * ty)
        pairs.append((device(i, c, zh, y), to))
    return pairs


def own_band_pairs():
    pairs = []
    for i, c, zh, y in everyone():
        stay = c == 0 and y % 2 == 1
        pairs.append((device(i, c, zh, y), device(i if stay else i + 1, c, zh, y)))
    return pairs


def next_band_pairs():
    pairs = []
    for i, c, zh, y in everyone():
        stay = c == 0 and y % 2 == 0
        pairs.append((device(i, c, zh, y), device(i if stay else i + 1, c, zh, y ^ 1)))
    return pairs


def core_pairs():
    return [(device(i, c, zh, y), device(i, 1 - c, zh, y)) for i, c, zh, y in everyone()]


def send(value, pairs):
    return lax.ppermute(value, ("i", "core", "band"), pairs)


def place():
    band = lax.axis_index("band")
    return lax.axis_index("i"), lax.axis_index("core"), band // 4, band % 4, band


def pick_kernel(index_ref, orb_ref, out_ref):
    for j in range(POINTS // 128):
        idx = jnp.broadcast_to(index_ref[:, j * 128 : (j + 1) * 128], (8, 128)) & 127
        low = lax.broadcasted_iota(jnp.int32, (8, 128), 1) < 64
        for part in range(2):
            left = orb_ref[:, part, 2 * j * 128 : (2 * j + 1) * 128]
            right = orb_ref[:, part, (2 * j + 1) * 128 : (2 * j + 2) * 128]
            got = jnp.where(
                low,
                jnp.take_along_axis(left, idx, axis=1, mode="promise_in_bounds"),
                jnp.take_along_axis(right, idx, axis=1, mode="promise_in_bounds"),
            )
            out_ref[part * 8 : part * 8 + 8, j * 128 : (j + 1) * 128] = got


def pick(orbitals, point_index):
    return pl.pallas_call(
        pick_kernel,
        out_shape=pltpu.VMEM((ROWS, POINTS), F32),
        name="pick_points",
    )(point_index.reshape(1, POINTS), orbitals)


def split(value):
    high = value.astype(BF16)
    return high, (value - high.astype(F32)).astype(BF16)


def product_kernel(core_ref, table_ref, occ_ref, weight_ref, *refs):
    k_refs, refs = refs[:WIDE], refs[WIDE:]
    mine, theirs, before = refs[0], refs[1], refs[2:6]
    high_ref, low_ref, p_ref, pt_ref, f_ref = refs[6:]
    i, c, zh, y, band = place()
    parity = y % 2
    kpoint = 2 * i + parity
    same = c == parity
    own_step = jnp.where(same, 2, 1)
    points = [lax.rem(kpoint - s + KPTS, KPTS) for s in (0, own_step, 3 - own_step)]

    @pl.when(pl.program_id(0) == 0)
    def _():
        f_ref[...] = jnp.zeros_like(f_ref)
        for g in range(STEPS):
            f_ref[pl.ds(g, 1), :] = weight_ref[pl.ds(table_ref[kpoint, points[g]], 1), :]
        p_ref[0:16, :] = jnp.where(same, mine[...], theirs[...])
        p_ref[16:32, :] = jnp.where(same, theirs[...], mine[...])
        for n in range(4):
            p_ref[32 + 16 * n : 48 + 16 * n, :] = before[n][...]
        for j in range(POINTS // 128):
            cols = slice(j * 128, (j + 1) * 128)
            scaled = jnp.concatenate([p_ref[32 * g : 32 * g + 32, cols] * f_ref[g : g + 1, cols] for g in range(STEPS)], axis=0)
            high = scaled.astype(BF16).astype(F32)
            pt_ref[cols, :] = jnp.concatenate([high, high, (scaled - high)[0:64]], axis=0).T.astype(BF16)

    row = lax.broadcasted_iota(jnp.int32, (32, 128), 0)
    number = jnp.where(row < 16, band, band ^ 1) * 8 + (row & 7)
    sides = []
    for j in range(WIDE):
        here = pl.ds(pl.multiple_of((2 * (pl.program_id(0) * WIDE + j) + c) * 128, 128), 128)
        f_here = f_ref[:, here]
        plain, turned = [], []
        for g in range(STEPS):
            live = number < occ_ref[points[g]]
            value = jnp.where(live, p_ref[32 * g : 32 * g + 32, here] * f_here[g : g + 1], 0.0)
            plain.append(value)
            turned += [value[8:16], -value[0:8], value[24:32], -value[16:24]]
        sides += [jnp.concatenate(plain, axis=0), jnp.concatenate(turned, axis=0)]
    high, low = split(jnp.concatenate(sides, axis=1))
    w = jnp.concatenate([high, low, high[0:64]], axis=0)
    for n in range(POINTS // CHUNK):
        rows = slice(n * CHUNK, (n + 1) * CHUNK)
        e = jnp.dot(pt_ref[rows, :], w, preferred_element_type=F32)
        for j in range(WIDE):
            kf = k_refs[j][rows, :].astype(F32)
            for part in range(2):
                cols = slice((2 * j + part) * 128, (2 * j + part + 1) * 128)
                high, low = split(e[:, cols] * kf)
                high_ref[pl.program_id(0), rows, cols] = high
                low_ref[pl.program_id(0), rows, cols] = low


WHOLE = pl.BlockSpec(memory_space=pltpu.VMEM)
SMEM = pl.BlockSpec(memory_space=pltpu.SMEM)


def product(core, q_table, occ_count, q_weight, kernel, mine, theirs, before):
    return pl.pallas_call(
        product_kernel,
        grid_spec=pltpu.PrefetchScalarGridSpec(
            num_scalar_prefetch=1,
            grid=(TILES,),
            in_specs=[SMEM, SMEM, WHOLE]
            + [pl.BlockSpec((POINTS, 128), lambda u, core, j=j: (0, 2 * (u * WIDE + j) + core[0])) for j in range(WIDE)]
            + [WHOLE] * 6,
            out_specs=[WHOLE, WHOLE],
            scratch_shapes=[
                pltpu.VMEM((32 * STEPS, POINTS), F32),
                pltpu.VMEM((POINTS, DEPTH), BF16),
                pltpu.VMEM((8, POINTS), F32),
            ],
        ),
        out_shape=[jax.ShapeDtypeStruct((TILES, POINTS, WIDE * 256), BF16)] * 2,
        compiler_params=pltpu.CompilerParams(vmem_limit_bytes=28 * 2**20),
        cost_estimate=pl.CostEstimate(flops=7 * 10**9, bytes_accessed=8 * 2**20, transcendentals=0),
        name="kernel_product",
    )(core, q_table, occ_count, q_weight, *[kernel] * WIDE, mine, theirs, *before)


def apply_kernel(high_ref, low_ref, *refs):
    mine, theirs, out_ref, x_ref = refs[0:4], refs[4:8], refs[8], refs[9]
    i, c, zh, y, band = place()
    same = c == y % 2
    for group, first in ((mine, jnp.where(same, band, band ^ 1)), (theirs, jnp.where(same, band ^ 1, band))):
        for t, ref in enumerate(group):
            block = first ^ (4 * (t // 2) + 2 * (t % 2))
            high, low = split(ref[...])
            row = pl.multiple_of(block * ROWS, ROWS)
            x_ref[pl.ds(row, ROWS), :] = high
            x_ref[pl.ds(pl.multiple_of(128 + row, ROWS), ROWS), :] = low
    for u in range(TILES):
        first = jnp.dot(x_ref[...], high_ref[u], preferred_element_type=F32)
        second = jnp.dot(x_ref[0:128, :], low_ref[u], preferred_element_type=F32)
        r = first[0:128] + first[128:256] + second
        for b in range(BLOCKS):
            top, bottom = r[b * ROWS : b * ROWS + 8], r[b * ROWS + 8 : b * ROWS + 16]
            for j in range(WIDE):
                re, im = slice(j * 256, j * 256 + 128), slice(j * 256 + 128, j * 256 + 256)
                out_ref[u * WIDE + j, b, 0] = top[:, re] - bottom[:, im]
                out_ref[u * WIDE + j, b, 1] = top[:, im] + bottom[:, re]


def apply(high, low, mine, theirs):
    return pl.pallas_call(
        apply_kernel,
        in_specs=[WHOLE] * 10,
        out_specs=WHOLE,
        out_shape=jax.ShapeDtypeStruct((TILES * WIDE, BLOCKS, 2, 8, 128), F32),
        scratch_shapes=[pltpu.VMEM((256, POINTS), BF16)],
        compiler_params=pltpu.CompilerParams(vmem_limit_bytes=28 * 2**20),
        cost_estimate=pl.CostEstimate(flops=4 * 10**9, bytes_accessed=18 * 2**20, transcendentals=0),
        name="apply_orbitals",
    )(high, low, *mine, *theirs)


def total_kernel(in_ref, out_ref):
    for k in range(KPTS):
        i, parity = k // 2, k % 2
        for part in range(2):
            parts = [in_ref[i * BLOCKS + zh * 4 + parity + 2 * h, part] for zh in range(2) for h in range(2)]
            out_ref[k, :, part, :] = ((parts[0] + parts[1]) + (parts[2] + parts[3])) * FACTOR


def total(parts):
    return pl.pallas_call(
        total_kernel,
        out_shape=jax.ShapeDtypeStruct((KPTS, 8, 2, 128), F32),
        name="total",
    )(pltpu.with_memory_space_constraint(parts, pltpu.VMEM))


def body(orbitals, point_index, kernel, q_weight, q_table, occ_count):
    core = lax.axis_index("core").astype(jnp.int32).reshape(1)
    kernel, q_weight, q_table, occ_count = (
        pltpu.with_memory_space_constraint(value, pltpu.HBM) for value in (kernel, q_weight, q_table, occ_count)
    )
    block = pick(orbitals[0], point_index)
    far = [send(block, gather_pairs(1, t)) for t in range(2)]
    near = [send(block, gather_pairs(0, t)) for t in range(2)]
    before = [send(block, own_band_pairs()), send(block, next_band_pairs())]
    before_theirs = [send(value, core_pairs()) for value in before]
    near_theirs = [send(value, core_pairs()) for value in near]
    high, low = product(core, q_table, occ_count, q_weight, kernel, near[0], near_theirs[0], before + before_theirs)
    far[0], far[1], high, low = lax.optimization_barrier((far[0], far[1], high, low))
    far_theirs = [send(value, core_pairs()) for value in far]
    parts = apply(high, low, near + far, near_theirs + far_theirs)
    got = lax.all_to_all(parts.reshape(64, 2, 8, 128), ("i", "band"), 0, 0, tiled=True)
    return total(got)


def solution(mesh):
    split_mesh = Mesh(mesh.devices.reshape(8, 2, BLOCKS), ("i", "core", "band"))
    ka = ("i", "core")
    placed = (P(ka, "band", None, None), P(), P(), P(), P(), P())
    return jax.shard_map(body, mesh=split_mesh, in_specs=placed, out_specs=P(None, "band", None, ka), check_vma=False)
```

```python
import jax
import jax.numpy as jnp
from jax import lax
from jax.experimental import pallas as pl
from jax.experimental.pallas import tpu as pltpu
from jax.sharding import Mesh
from jax.sharding import PartitionSpec as P

STEPS = 3
KPTS = 16
BLOCKS = 8
ROWS = 16
POINTS = 2048
TILES = 4
WIDE = 2
DEPTH = 256
CHUNK = 512
FACTOR = -1.0 / (STEPS * 64) ** 0.5
F32, BF16 = jnp.float32, jnp.bfloat16


def device(i, c, zh, y):
    return ((i % 8) * 2 + c) * BLOCKS + zh * 4 + y % 4


def everyone():
    return [(i, c, zh, y) for i in range(8) for c in range(2) for zh in range(2) for y in range(4)]


def gather_pairs(tz, ty):
    pairs = []
    for i, c, zh, y in everyone():
        if y % 2 == c:
            to = device(i, c, zh ^ tz, y + 2 * ty)
        else:
            to = device(i, 1 - c, zh ^ tz, (y ^ 1) + 2 * ty)
        pairs.append((device(i, c, zh, y), to))
    return pairs


def own_band_pairs():
    pairs = []
    for i, c, zh, y in everyone():
        stay = c == 0 and y % 2 == 1
        pairs.append((device(i, c, zh, y), device(i if stay else i + 1, c, zh, y)))
    return pairs


def next_band_pairs():
    pairs = []
    for i, c, zh, y in everyone():
        stay = c == 0 and y % 2 == 0
        pairs.append((device(i, c, zh, y), device(i if stay else i + 1, c, zh, y ^ 1)))
    return pairs


def core_pairs():
    return [(device(i, c, zh, y), device(i, 1 - c, zh, y)) for i, c, zh, y in everyone()]


def send(value, pairs):
    return lax.ppermute(value, ("i", "core", "band"), pairs)


def place():
    band = lax.axis_index("band")
    return lax.axis_index("i"), lax.axis_index("core"), band // 4, band % 4, band


def pick_kernel(index_ref, orb_ref, out_ref):
    for j in range(POINTS // 128):
        idx = jnp.broadcast_to(index_ref[:, j * 128 : (j + 1) * 128], (8, 128)) & 127
        low = lax.broadcasted_iota(jnp.int32, (8, 128), 1) < 64
        for part in range(2):
            left = orb_ref[:, part, 2 * j * 128 : (2 * j + 1) * 128]
            right = orb_ref[:, part, (2 * j + 1) * 128 : (2 * j + 2) * 128]
            got = jnp.where(
                low,
                jnp.take_along_axis(left, idx, axis=1, mode="promise_in_bounds"),
                jnp.take_along_axis(right, idx, axis=1, mode="promise_in_bounds"),
            )
            out_ref[part * 8 : part * 8 + 8, j * 128 : (j + 1) * 128] = got


def pick(orbitals, point_index):
    return pl.pallas_call(
        pick_kernel,
        out_shape=pltpu.VMEM((ROWS, POINTS), F32),
        name="pick_points",
    )(point_index.reshape(1, POINTS), orbitals)


def split(value):
    high = value.astype(BF16)
    return high, (value - high.astype(F32)).astype(BF16)


def product_kernel(core_ref, table_ref, occ_ref, weight_ref, *refs):
    k_refs, refs = refs[:WIDE], refs[WIDE:]
    mine, theirs, before = refs[0], refs[1], refs[2:6]
    high_ref, low_ref, p_ref, pt_ref, f_ref = refs[6:]
    i, c, zh, y, band = place()
    parity = y % 2
    kpoint = 2 * i + parity
    same = c == parity
    own_step = jnp.where(same, 2, 1)
    points = [lax.rem(kpoint - s + KPTS, KPTS) for s in (0, own_step, 3 - own_step)]

    @pl.when(pl.program_id(0) == 0)
    def _():
        f_ref[...] = jnp.zeros_like(f_ref)
        for g in range(STEPS):
            f_ref[pl.ds(g, 1), :] = weight_ref[pl.ds(table_ref[kpoint, points[g]], 1), :]
        p_ref[0:16, :] = jnp.where(same, mine[...], theirs[...])
        p_ref[16:32, :] = jnp.where(same, theirs[...], mine[...])
        for n in range(4):
            p_ref[32 + 16 * n : 48 + 16 * n, :] = before[n][...]
        for j in range(POINTS // 128):
            cols = slice(j * 128, (j + 1) * 128)
            scaled = jnp.concatenate([p_ref[32 * g : 32 * g + 32, cols] * f_ref[g : g + 1, cols] for g in range(STEPS)], axis=0)
            high = scaled.astype(BF16).astype(F32)
            pt_ref[cols, :] = jnp.concatenate([high, high, (scaled - high)[0:64]], axis=0).T.astype(BF16)

    row = lax.broadcasted_iota(jnp.int32, (32, 128), 0)
    number = jnp.where(row < 16, band, band ^ 1) * 8 + (row & 7)
    sides = []
    for j in range(WIDE):
        here = pl.ds(pl.multiple_of((2 * (pl.program_id(0) * WIDE + j) + c) * 128, 128), 128)
        f_here = f_ref[:, here]
        plain, turned = [], []
        for g in range(STEPS):
            live = number < occ_ref[points[g]]
            value = jnp.where(live, p_ref[32 * g : 32 * g + 32, here] * f_here[g : g + 1], 0.0)
            plain.append(value)
            turned += [value[8:16], -value[0:8], value[24:32], -value[16:24]]
        sides += [jnp.concatenate(plain, axis=0), jnp.concatenate(turned, axis=0)]
    high, low = split(jnp.concatenate(sides, axis=1))
    w = jnp.concatenate([high, low, high[0:64]], axis=0)
    for n in range(POINTS // CHUNK):
        rows = slice(n * CHUNK, (n + 1) * CHUNK)
        e = jnp.dot(pt_ref[rows, :], w, preferred_element_type=F32)
        for j in range(WIDE):
            kf = k_refs[j][rows, :].astype(F32)
            for part in range(2):
                cols = slice((2 * j + part) * 128, (2 * j + part + 1) * 128)
                high, low = split(e[:, cols] * kf)
                high_ref[pl.program_id(0), rows, cols] = high
                low_ref[pl.program_id(0), rows, cols] = low


WHOLE = pl.BlockSpec(memory_space=pltpu.VMEM)
SMEM = pl.BlockSpec(memory_space=pltpu.SMEM)


def product(core, q_table, occ_count, q_weight, kernel, mine, theirs, before):
    return pl.pallas_call(
        product_kernel,
        grid_spec=pltpu.PrefetchScalarGridSpec(
            num_scalar_prefetch=1,
            grid=(TILES,),
            in_specs=[SMEM, SMEM, WHOLE]
            + [pl.BlockSpec((POINTS, 128), lambda u, core, j=j: (0, 2 * (u * WIDE + j) + core[0])) for j in range(WIDE)]
            + [WHOLE] * 6,
            out_specs=[WHOLE, WHOLE],
            scratch_shapes=[
                pltpu.VMEM((32 * STEPS, POINTS), F32),
                pltpu.VMEM((POINTS, DEPTH), BF16),
                pltpu.VMEM((8, POINTS), F32),
            ],
        ),
        out_shape=[jax.ShapeDtypeStruct((TILES, POINTS, WIDE * 256), BF16)] * 2,
        compiler_params=pltpu.CompilerParams(vmem_limit_bytes=28 * 2**20),
        cost_estimate=pl.CostEstimate(flops=7 * 10**9, bytes_accessed=8 * 2**20, transcendentals=0),
        name="kernel_product",
    )(core, q_table, occ_count, q_weight, *[kernel] * WIDE, mine, theirs, *before)


def apply_kernel(high_ref, low_ref, *refs):
    mine, theirs, out_ref, x_ref = refs[0:4], refs[4:8], refs[8], refs[9]
    i, c, zh, y, band = place()
    same = c == y % 2
    for group, first in ((mine, jnp.where(same, band, band ^ 1)), (theirs, jnp.where(same, band ^ 1, band))):
        for t, ref in enumerate(group):
            block = first ^ (4 * (t // 2) + 2 * (t % 2))
            high, low = split(ref[...])
            row = pl.multiple_of(block * ROWS, ROWS)
            x_ref[pl.ds(row, ROWS), :] = high
            x_ref[pl.ds(pl.multiple_of(128 + row, ROWS), ROWS), :] = low
    for u in range(TILES):
        first = jnp.dot(x_ref[...], high_ref[u], preferred_element_type=F32)
        second = jnp.dot(x_ref[0:128, :], low_ref[u], preferred_element_type=F32)
        r = first[0:128] + first[128:256] + second
        for b in range(BLOCKS):
            top, bottom = r[b * ROWS : b * ROWS + 8], r[b * ROWS + 8 : b * ROWS + 16]
            for j in range(WIDE):
                re, im = slice(j * 256, j * 256 + 128), slice(j * 256 + 128, j * 256 + 256)
                out_ref[u * WIDE + j, b, 0] = top[:, re] - bottom[:, im]
                out_ref[u * WIDE + j, b, 1] = top[:, im] + bottom[:, re]


def apply(high, low, mine, theirs):
    return pl.pallas_call(
        apply_kernel,
        in_specs=[WHOLE] * 10,
        out_specs=WHOLE,
        out_shape=jax.ShapeDtypeStruct((TILES * WIDE, BLOCKS, 2, 8, 128), F32),
        scratch_shapes=[pltpu.VMEM((256, POINTS), BF16)],
        compiler_params=pltpu.CompilerParams(vmem_limit_bytes=28 * 2**20),
        cost_estimate=pl.CostEstimate(flops=4 * 10**9, bytes_accessed=18 * 2**20, transcendentals=0),
        name="apply_orbitals",
    )(high, low, *mine, *theirs)


def total_kernel(in_ref, out_ref):
    for k in range(KPTS):
        i, parity = k // 2, k % 2
        for part in range(2):
            parts = [in_ref[i * BLOCKS + zh * 4 + parity + 2 * h, part] for zh in range(2) for h in range(2)]
            out_ref[k, :, part, :] = ((parts[0] + parts[1]) + (parts[2] + parts[3])) * FACTOR


def total(parts):
    return pl.pallas_call(
        total_kernel,
        out_shape=jax.ShapeDtypeStruct((KPTS, 8, 2, 128), F32),
        name="total",
    )(pltpu.with_memory_space_constraint(parts, pltpu.VMEM))


def body(orbitals, point_index, kernel, q_weight, q_table, occ_count):
    core = lax.axis_index("core").astype(jnp.int32).reshape(1)
    kernel, q_weight, q_table, occ_count = (
        pltpu.with_memory_space_constraint(value, pltpu.HBM) for value in (kernel, q_weight, q_table, occ_count)
    )
    block = pick(orbitals[0], point_index)
    far = [send(block, gather_pairs(1, t)) for t in (1, 0)][::-1]
    near = [send(block, gather_pairs(0, t)) for t in range(2)]
    before = [send(block, own_band_pairs()), send(block, next_band_pairs())]
    before_theirs = [send(value, core_pairs()) for value in before]
    near_theirs = [send(value, core_pairs()) for value in near]
    high, low = product(core, q_table, occ_count, q_weight, kernel, near[0], near_theirs[0], before + before_theirs)
    far[1], high, low = lax.optimization_barrier((far[1], high, low))
    far_theirs = [send(value, core_pairs()) for value in far]
    parts = apply(high, low, near + far, near_theirs + far_theirs)
    got = lax.all_to_all(parts.reshape(64, 2, 8, 128), ("i", "band"), 0, 0, tiled=True)
    return total(got)


def solution(mesh):
    split_mesh = Mesh(mesh.devices.reshape(8, 2, BLOCKS), ("i", "core", "band"))
    ka = ("i", "core")
    placed = (P(ka, "band", None, None), P(), P(), P(), P(), P())
    return jax.shard_map(body, mesh=split_mesh, in_specs=placed, out_specs=P(None, "band", None, ka), check_vma=False)
```

```python
import jax
import jax.numpy as jnp
from jax import lax
from jax.experimental import pallas as pl
from jax.experimental.pallas import tpu as pltpu
from jax.sharding import Mesh
from jax.sharding import PartitionSpec as P

STEPS = 3
KPTS = 16
BLOCKS = 8
ROWS = 16
POINTS = 2048
TILES = 4
WIDE = 2
DEPTH = 256
CHUNK = 512
FACTOR = -1.0 / (STEPS * 64) ** 0.5
F32, BF16 = jnp.float32, jnp.bfloat16


def device(i, c, zh, y):
    return ((i % 8) * 2 + c) * BLOCKS + zh * 4 + y % 4


def everyone():
    return [(i, c, zh, y) for i in range(8) for c in range(2) for zh in range(2) for y in range(4)]


def gather_pairs(tz, ty):
    pairs = []
    for i, c, zh, y in everyone():
        if y % 2 == c:
            to = device(i, c, zh ^ tz, y + 2 * ty)
        else:
            to = device(i, 1 - c, zh ^ tz, (y ^ 1) + 2 * ty)
        pairs.append((device(i, c, zh, y), to))
    return pairs


def own_band_pairs():
    pairs = []
    for i, c, zh, y in everyone():
        stay = c == 0 and y % 2 == 1
        pairs.append((device(i, c, zh, y), device(i if stay else i + 1, c, zh, y)))
    return pairs


def next_band_pairs():
    pairs = []
    for i, c, zh, y in everyone():
        stay = c == 0 and y % 2 == 0
        pairs.append((device(i, c, zh, y), device(i if stay else i + 1, c, zh, y ^ 1)))
    return pairs


def core_pairs():
    return [(device(i, c, zh, y), device(i, 1 - c, zh, y)) for i, c, zh, y in everyone()]


def send(value, pairs):
    return lax.ppermute(value, ("i", "core", "band"), pairs)


def place():
    band = lax.axis_index("band")
    return lax.axis_index("i"), lax.axis_index("core"), band // 4, band % 4, band


def pick_kernel(index_ref, orb_ref, out_ref):
    for j in range(POINTS // 128):
        idx = jnp.broadcast_to(index_ref[:, j * 128 : (j + 1) * 128], (8, 128)) & 127
        low = lax.broadcasted_iota(jnp.int32, (8, 128), 1) < 64
        for part in range(2):
            left = orb_ref[:, part, 2 * j * 128 : (2 * j + 1) * 128]
            right = orb_ref[:, part, (2 * j + 1) * 128 : (2 * j + 2) * 128]
            got = jnp.where(
                low,
                jnp.take_along_axis(left, idx, axis=1, mode="promise_in_bounds"),
                jnp.take_along_axis(right, idx, axis=1, mode="promise_in_bounds"),
            )
            out_ref[part * 8 : part * 8 + 8, j * 128 : (j + 1) * 128] = got


def pick(orbitals, point_index):
    return pl.pallas_call(
        pick_kernel,
        out_shape=pltpu.VMEM((ROWS, POINTS), F32),
        name="pick_points",
    )(point_index.reshape(1, POINTS), orbitals)


def split(value):
    high = value.astype(BF16)
    return high, (value - high.astype(F32)).astype(BF16)


def product_kernel(table_ref, occ_ref, weight_ref, *refs):
    k_refs, refs = refs[:WIDE], refs[WIDE:]
    mine, theirs, before = refs[0], refs[1], refs[2:6]
    high_ref, low_ref, p_ref, pt_ref, f_ref = refs[6:]
    i, c, zh, y, band = place()
    parity = y % 2
    kpoint = 2 * i + parity
    same = c == parity
    own_step = jnp.where(same, 2, 1)
    points = [lax.rem(kpoint - s + KPTS, KPTS) for s in (0, own_step, 3 - own_step)]

    @pl.when(pl.program_id(0) == 0)
    def _():
        f_ref[...] = jnp.zeros_like(f_ref)
        for g in range(STEPS):
            f_ref[pl.ds(g, 1), :] = weight_ref[pl.ds(table_ref[kpoint, points[g]], 1), :]
        p_ref[0:16, :] = jnp.where(same, mine[...], theirs[...])
        p_ref[16:32, :] = jnp.where(same, theirs[...], mine[...])
        for n in range(4):
            p_ref[32 + 16 * n : 48 + 16 * n, :] = before[n][...]
        for j in range(POINTS // 128):
            cols = slice(j * 128, (j + 1) * 128)
            scaled = jnp.concatenate([p_ref[32 * g : 32 * g + 32, cols] * f_ref[g : g + 1, cols] for g in range(STEPS)], axis=0)
            high = scaled.astype(BF16).astype(F32)
            pt_ref[cols, :] = jnp.concatenate([high, high, (scaled - high)[0:64]], axis=0).T.astype(BF16)

    row = lax.broadcasted_iota(jnp.int32, (32, 128), 0)
    number = jnp.where(row < 16, band, band ^ 1) * 8 + (row & 7)
    sides = []
    for j in range(WIDE):
        here = pl.ds(pl.multiple_of((2 * (pl.program_id(0) * WIDE + j) + c) * 128, 128), 128)
        f_here = f_ref[:, here]
        plain, turned = [], []
        for g in range(STEPS):
            live = number < occ_ref[points[g]]
            value = jnp.where(live, p_ref[32 * g : 32 * g + 32, here] * f_here[g : g + 1], 0.0)
            plain.append(value)
            turned += [value[8:16], -value[0:8], value[24:32], -value[16:24]]
        sides += [jnp.concatenate(plain, axis=0), jnp.concatenate(turned, axis=0)]
    high, low = split(jnp.concatenate(sides, axis=1))
    w = jnp.concatenate([high, low, high[0:64]], axis=0)
    for n in range(POINTS // CHUNK):
        rows = slice(n * CHUNK, (n + 1) * CHUNK)
        e = jnp.dot(pt_ref[rows, :], w, preferred_element_type=F32)
        for j in range(WIDE):
            kf = k_refs[j][rows, :].astype(F32)
            for part in range(2):
                cols = slice((2 * j + part) * 128, (2 * j + part + 1) * 128)
                high, low = split(e[:, cols] * kf)
                high_ref[pl.program_id(0), rows, cols] = high
                low_ref[pl.program_id(0), rows, cols] = low


WHOLE = pl.BlockSpec(memory_space=pltpu.VMEM)
SMEM = pl.BlockSpec(memory_space=pltpu.SMEM)


def product(q_table, occ_count, q_weight, kernel, mine, theirs, before):
    return pl.pallas_call(
        product_kernel,
        grid_spec=pltpu.PrefetchScalarGridSpec(
            num_scalar_prefetch=0,
            grid=(TILES,),
            in_specs=[SMEM, SMEM, WHOLE]
            + [pl.BlockSpec((POINTS, 128), lambda u, j=j: (0, 2 * (u * WIDE + j) + lax.axis_index("core"))) for j in range(WIDE)]
            + [WHOLE] * 6,
            out_specs=[WHOLE, WHOLE],
            scratch_shapes=[
                pltpu.VMEM((32 * STEPS, POINTS), F32),
                pltpu.VMEM((POINTS, DEPTH), BF16),
                pltpu.VMEM((8, POINTS), F32),
            ],
        ),
        out_shape=[jax.ShapeDtypeStruct((TILES, POINTS, WIDE * 256), BF16)] * 2,
        compiler_params=pltpu.CompilerParams(vmem_limit_bytes=28 * 2**20),
        cost_estimate=pl.CostEstimate(flops=7 * 10**9, bytes_accessed=8 * 2**20, transcendentals=0),
        name="kernel_product",
    )(q_table, occ_count, q_weight, *[kernel] * WIDE, mine, theirs, *before)


def apply_kernel(high_ref, low_ref, *refs):
    mine, theirs, out_ref, x_ref = refs[0:4], refs[4:8], refs[8], refs[9]
    i, c, zh, y, band = place()
    same = c == y % 2
    for group, first in ((mine, jnp.where(same, band, band ^ 1)), (theirs, jnp.where(same, band ^ 1, band))):
        for t, ref in enumerate(group):
            block = first ^ (4 * (t // 2) + 2 * (t % 2))
            high, low = split(ref[...])
            row = pl.multiple_of(block * ROWS, ROWS)
            x_ref[pl.ds(row, ROWS), :] = high
            x_ref[pl.ds(pl.multiple_of(128 + row, ROWS), ROWS), :] = low
    for u in range(TILES):
        first = jnp.dot(x_ref[...], high_ref[u], preferred_element_type=F32)
        second = jnp.dot(x_ref[0:128, :], low_ref[u], preferred_element_type=F32)
        r = first[0:128] + first[128:256] + second
        for b in range(BLOCKS):
            top, bottom = r[b * ROWS : b * ROWS + 8], r[b * ROWS + 8 : b * ROWS + 16]
            for j in range(WIDE):
                re, im = slice(j * 256, j * 256 + 128), slice(j * 256 + 128, j * 256 + 256)
                out_ref[u * WIDE + j, b, 0] = top[:, re] - bottom[:, im]
                out_ref[u * WIDE + j, b, 1] = top[:, im] + bottom[:, re]


def apply(high, low, mine, theirs):
    return pl.pallas_call(
        apply_kernel,
        in_specs=[WHOLE] * 10,
        out_specs=WHOLE,
        out_shape=jax.ShapeDtypeStruct((TILES * WIDE, BLOCKS, 2, 8, 128), F32),
        scratch_shapes=[pltpu.VMEM((256, POINTS), BF16)],
        compiler_params=pltpu.CompilerParams(vmem_limit_bytes=28 * 2**20),
        cost_estimate=pl.CostEstimate(flops=4 * 10**9, bytes_accessed=18 * 2**20, transcendentals=0),
        name="apply_orbitals",
    )(high, low, *mine, *theirs)


def total_kernel(in_ref, out_ref):
    for k in range(KPTS):
        i, parity = k // 2, k % 2
        for part in range(2):
            parts = [in_ref[i * BLOCKS + zh * 4 + parity + 2 * h, part] for zh in range(2) for h in range(2)]
            out_ref[k, :, part, :] = ((parts[0] + parts[1]) + (parts[2] + parts[3])) * FACTOR


def total(parts):
    return pl.pallas_call(
        total_kernel,
        out_shape=jax.ShapeDtypeStruct((KPTS, 8, 2, 128), F32),
        name="total",
    )(pltpu.with_memory_space_constraint(parts, pltpu.VMEM))


def body(orbitals, point_index, kernel, q_weight, q_table, occ_count):
    kernel, q_weight, q_table, occ_count = (
        pltpu.with_memory_space_constraint(value, pltpu.HBM) for value in (kernel, q_weight, q_table, occ_count)
    )
    block = pick(orbitals[0], point_index)
    far = [send(block, gather_pairs(1, t)) for t in (1, 0)][::-1]
    near = [send(block, gather_pairs(0, t)) for t in range(2)]
    before = [send(block, own_band_pairs()), send(block, next_band_pairs())]
    before_theirs = [send(value, core_pairs()) for value in before]
    near_theirs = [send(value, core_pairs()) for value in near]
    high, low = product(q_table, occ_count, q_weight, kernel, near[0], near_theirs[0], before + before_theirs)
    far[1], high, low = lax.optimization_barrier((far[1], high, low))
    far_theirs = [send(value, core_pairs()) for value in far]
    parts = apply(high, low, near + far, near_theirs + far_theirs)
    got = lax.all_to_all(parts.reshape(64, 2, 8, 128), ("i", "band"), 0, 0, tiled=True)
    return total(got)


def solution(mesh):
    split_mesh = Mesh(mesh.devices.reshape(8, 2, BLOCKS), ("i", "core", "band"))
    ka = ("i", "core")
    placed = (P(ka, "band", None, None), P(), P(), P(), P(), P())
    return jax.shard_map(body, mesh=split_mesh, in_specs=placed, out_specs=P(None, "band", None, ka), check_vma=False)
```

```python
import jax
import jax.numpy as jnp
from jax import lax
from jax.experimental import pallas as pl
from jax.experimental.pallas import tpu as pltpu
from jax.sharding import Mesh
from jax.sharding import PartitionSpec as P

STEPS = 3
KPTS = 16
BLOCKS = 8
ROWS = 16
POINTS = 2048
TILES = 4
WIDE = 2
DEPTH = 256
CHUNK = 1024
FACTOR = -1.0 / (STEPS * 64) ** 0.5
F32, BF16 = jnp.float32, jnp.bfloat16


def device(i, c, zh, y):
    return ((i % 8) * 2 + c) * BLOCKS + zh * 4 + y % 4


def everyone():
    return [(i, c, zh, y) for i in range(8) for c in range(2) for zh in range(2) for y in range(4)]


def gather_pairs(tz, ty):
    pairs = []
    for i, c, zh, y in everyone():
        if y % 2 == c:
            to = device(i, c, zh ^ tz, y + 2 * ty)
        else:
            to = device(i, 1 - c, zh ^ tz, (y ^ 1) + 2 * ty)
        pairs.append((device(i, c, zh, y), to))
    return pairs


def own_band_pairs():
    pairs = []
    for i, c, zh, y in everyone():
        stay = c == 0 and y % 2 == 1
        pairs.append((device(i, c, zh, y), device(i if stay else i + 1, c, zh, y)))
    return pairs


def next_band_pairs():
    pairs = []
    for i, c, zh, y in everyone():
        stay = c == 0 and y % 2 == 0
        pairs.append((device(i, c, zh, y), device(i if stay else i + 1, c, zh, y ^ 1)))
    return pairs


def core_pairs():
    return [(device(i, c, zh, y), device(i, 1 - c, zh, y)) for i, c, zh, y in everyone()]


def send(value, pairs):
    return lax.ppermute(value, ("i", "core", "band"), pairs)


def place():
    band = lax.axis_index("band")
    return lax.axis_index("i"), lax.axis_index("core"), band // 4, band % 4, band


def pick_kernel(index_ref, orb_ref, out_ref):
    for j in range(POINTS // 128):
        idx = jnp.broadcast_to(index_ref[:, j * 128 : (j + 1) * 128], (8, 128)) & 127
        low = lax.broadcasted_iota(jnp.int32, (8, 128), 1) < 64
        for part in range(2):
            left = orb_ref[:, part, 2 * j * 128 : (2 * j + 1) * 128]
            right = orb_ref[:, part, (2 * j + 1) * 128 : (2 * j + 2) * 128]
            got = jnp.where(
                low,
                jnp.take_along_axis(left, idx, axis=1, mode="promise_in_bounds"),
                jnp.take_along_axis(right, idx, axis=1, mode="promise_in_bounds"),
            )
            out_ref[part * 8 : part * 8 + 8, j * 128 : (j + 1) * 128] = got


def pick(orbitals, point_index):
    return pl.pallas_call(
        pick_kernel,
        out_shape=pltpu.VMEM((ROWS, POINTS), F32),
        name="pick_points",
    )(point_index.reshape(1, POINTS), orbitals)


def split(value):
    high = value.astype(BF16)
    return high, (value - high.astype(F32)).astype(BF16)


def product_kernel(core_ref, table_ref, occ_ref, weight_ref, *refs):
    k_refs, refs = refs[:WIDE], refs[WIDE:]
    mine, theirs, before = refs[0], refs[1], refs[2:6]
    high_ref, low_ref, p_ref, pt_ref, f_ref = refs[6:]
    i, c, zh, y, band = place()
    parity = y % 2
    kpoint = 2 * i + parity
    same = c == parity
    own_step = jnp.where(same, 2, 1)
    points = [lax.rem(kpoint - s + KPTS, KPTS) for s in (0, own_step, 3 - own_step)]

    @pl.when(pl.program_id(0) == 0)
    def _():
        f_ref[...] = jnp.zeros_like(f_ref)
        for g in range(STEPS):
            f_ref[pl.ds(g, 1), :] = weight_ref[pl.ds(table_ref[kpoint, points[g]], 1), :]
        p_ref[0:16, :] = jnp.where(same, mine[...], theirs[...])
        p_ref[16:32, :] = jnp.where(same, theirs[...], mine[...])
        for n in range(4):
            p_ref[32 + 16 * n : 48 + 16 * n, :] = before[n][...]
        for j in range(POINTS // 128):
            cols = slice(j * 128, (j + 1) * 128)
            scaled = jnp.concatenate([p_ref[32 * g : 32 * g + 32, cols] * f_ref[g : g + 1, cols] for g in range(STEPS)], axis=0)
            high = scaled.astype(BF16).astype(F32)
            pt_ref[cols, :] = jnp.concatenate([high, high, (scaled - high)[0:64]], axis=0).T.astype(BF16)

    row = lax.broadcasted_iota(jnp.int32, (32, 128), 0)
    number = jnp.where(row < 16, band, band ^ 1) * 8 + (row & 7)
    sides = []
    for j in range(WIDE):
        here = pl.ds(pl.multiple_of((2 * (pl.program_id(0) * WIDE + j) + c) * 128, 128), 128)
        f_here = f_ref[:, here]
        plain, turned = [], []
        for g in range(STEPS):
            live = number < occ_ref[points[g]]
            value = jnp.where(live, p_ref[32 * g : 32 * g + 32, here] * f_here[g : g + 1], 0.0)
            plain.append(value)
            turned += [value[8:16], -value[0:8], value[24:32], -value[16:24]]
        sides += [jnp.concatenate(plain, axis=0), jnp.concatenate(turned, axis=0)]
    high, low = split(jnp.concatenate(sides, axis=1))
    w = jnp.concatenate([high, low, high[0:64]], axis=0)
    for n in range(POINTS // CHUNK):
        rows = slice(n * CHUNK, (n + 1) * CHUNK)
        e = jnp.dot(pt_ref[rows, :], w, preferred_element_type=F32)
        for j in range(WIDE):
            kf = k_refs[j][rows, :].astype(F32)
            for part in range(2):
                cols = slice((2 * j + part) * 128, (2 * j + part + 1) * 128)
                high, low = split(e[:, cols] * kf)
                high_ref[pl.program_id(0), rows, cols] = high
                low_ref[pl.program_id(0), rows, cols] = low


WHOLE = pl.BlockSpec(memory_space=pltpu.VMEM)
SMEM = pl.BlockSpec(memory_space=pltpu.SMEM)


def product(core, q_table, occ_count, q_weight, kernel, mine, theirs, before):
    return pl.pallas_call(
        product_kernel,
        grid_spec=pltpu.PrefetchScalarGridSpec(
            num_scalar_prefetch=1,
            grid=(TILES,),
            in_specs=[SMEM, SMEM, WHOLE]
            + [pl.BlockSpec((POINTS, 128), lambda u, core, j=j: (0, 2 * (u * WIDE + j) + core[0])) for j in range(WIDE)]
            + [WHOLE] * 6,
            out_specs=[WHOLE, WHOLE],
            scratch_shapes=[
                pltpu.VMEM((32 * STEPS, POINTS), F32),
                pltpu.VMEM((POINTS, DEPTH), BF16),
                pltpu.VMEM((8, POINTS), F32),
            ],
        ),
        out_shape=[jax.ShapeDtypeStruct((TILES, POINTS, WIDE * 256), BF16)] * 2,
        compiler_params=pltpu.CompilerParams(vmem_limit_bytes=28 * 2**20),
        cost_estimate=pl.CostEstimate(flops=7 * 10**9, bytes_accessed=8 * 2**20, transcendentals=0),
        name="kernel_product",
    )(core, q_table, occ_count, q_weight, *[kernel] * WIDE, mine, theirs, *before)


def apply_kernel(high_ref, low_ref, *refs):
    mine, theirs, out_ref, x_ref = refs[0:4], refs[4:8], refs[8], refs[9]
    i, c, zh, y, band = place()
    same = c == y % 2
    for group, first in ((mine, jnp.where(same, band, band ^ 1)), (theirs, jnp.where(same, band ^ 1, band))):
        for t, ref in enumerate(group):
            block = first ^ (4 * (t // 2) + 2 * (t % 2))
            high, low = split(ref[...])
            row = pl.multiple_of(block * ROWS, ROWS)
            x_ref[pl.ds(row, ROWS), :] = high
            x_ref[pl.ds(pl.multiple_of(128 + row, ROWS), ROWS), :] = low
    for u in range(TILES):
        first = jnp.dot(x_ref[...], high_ref[u], preferred_element_type=F32)
        second = jnp.dot(x_ref[0:128, :], low_ref[u], preferred_element_type=F32)
        r = first[0:128] + first[128:256] + second
        for b in range(BLOCKS):
            top, bottom = r[b * ROWS : b * ROWS + 8], r[b * ROWS + 8 : b * ROWS + 16]
            for j in range(WIDE):
                re, im = slice(j * 256, j * 256 + 128), slice(j * 256 + 128, j * 256 + 256)
                out_ref[u * WIDE + j, b, 0] = top[:, re] - bottom[:, im]
                out_ref[u * WIDE + j, b, 1] = top[:, im] + bottom[:, re]


def apply(high, low, mine, theirs):
    return pl.pallas_call(
        apply_kernel,
        in_specs=[WHOLE] * 10,
        out_specs=WHOLE,
        out_shape=jax.ShapeDtypeStruct((TILES * WIDE, BLOCKS, 2, 8, 128), F32),
        scratch_shapes=[pltpu.VMEM((256, POINTS), BF16)],
        compiler_params=pltpu.CompilerParams(vmem_limit_bytes=28 * 2**20),
        cost_estimate=pl.CostEstimate(flops=4 * 10**9, bytes_accessed=18 * 2**20, transcendentals=0),
        name="apply_orbitals",
    )(high, low, *mine, *theirs)


def total_kernel(in_ref, out_ref):
    for k in range(KPTS):
        i, parity = k // 2, k % 2
        for part in range(2):
            parts = [in_ref[i * BLOCKS + zh * 4 + parity + 2 * h, part] for zh in range(2) for h in range(2)]
            out_ref[k, :, part, :] = ((parts[0] + parts[1]) + (parts[2] + parts[3])) * FACTOR


def total(parts):
    return pl.pallas_call(
        total_kernel,
        out_shape=jax.ShapeDtypeStruct((KPTS, 8, 2, 128), F32),
        name="total",
    )(pltpu.with_memory_space_constraint(parts, pltpu.VMEM))


def body(orbitals, point_index, kernel, q_weight, q_table, occ_count):
    core = lax.axis_index("core").astype(jnp.int32).reshape(1)
    kernel, q_weight, q_table, occ_count = (
        pltpu.with_memory_space_constraint(value, pltpu.HBM) for value in (kernel, q_weight, q_table, occ_count)
    )
    block = pick(orbitals[0], point_index)
    far = [send(block, gather_pairs(1, t)) for t in (1, 0)][::-1]
    near = [send(block, gather_pairs(0, t)) for t in range(2)]
    before = [send(block, pairs) for pairs in (next_band_pairs(), own_band_pairs())][::-1]
    before_theirs = [send(value, core_pairs()) for value in before]
    near_theirs = [send(value, core_pairs()) for value in near]
    high, low = product(core, q_table, occ_count, q_weight, kernel, near[0], near_theirs[0], before + before_theirs)
    far[1], high, low = lax.optimization_barrier((far[1], high, low))
    far_theirs = [send(value, core_pairs()) for value in far]
    parts = apply(high, low, near + far, near_theirs + far_theirs)
    got = lax.all_to_all(parts.reshape(64, 2, 8, 128), ("i", "band"), 0, 0, tiled=True)
    return total(got)


def solution(mesh):
    split_mesh = Mesh(mesh.devices.reshape(8, 2, BLOCKS), ("i", "core", "band"))
    ka = ("i", "core")
    placed = (P(ka, "band", None, None), P(), P(), P(), P(), P())
    return jax.shard_map(body, mesh=split_mesh, in_specs=placed, out_specs=P(None, "band", None, ka), check_vma=False)
```
